32 devices in a mesh: grp: 2 (over y), atoms: 4 (over z), vec: 2 (over x), sub: 2 (over core).
Axes of the slice: x: 2, y: 2, z: 4, core: 2. Of those that a mesh axis runs over, the one named last changes fastest.
Arguments:
- t_prev: float32 [256, 12288], P('grp', ('atoms', 'vec', 'sub')), parts along dimension 0, may hold values from -6 to 6
- t_cur: float32 [256, 12288], P('grp', ('atoms', 'vec', 'sub')), parts along dimension 0, may hold values from -6 to 6
- diag_blocks: bfloat16 [64, 384, 384], P(('grp', 'atoms', 'vec', 'sub')), parts along dimension 0, as said below
- upper_half_blocks: bfloat16 [320, 384, 384], P(('grp', 'atoms', 'vec', 'sub')), parts along dimension 0, may hold values from -0.046875 to 0.046875
- offsets: int32 [64, 5], P(('grp', 'atoms', 'vec', 'sub')), parts along dimension 0, may hold values from 1 to 8, as said below
Outputs:
- t_one: float32 [256, 12288], P('grp', ('atoms', 'vec', 'sub')), parts along dimension 0
- t_two: float32 [256, 12288], P('grp', ('atoms', 'vec', 'sub')), parts along dimension 0
The draws below stay inside these ranges and needn't reach their ends.
There are 2 independent parts, one for each index of `grp`. The reference program is written for one: setup_inputs(seed, part) draws one part's arguments, and reference() takes and returns one part's arrays. A program takes and returns all parts, laid end to end along the dimension named above; each array names one. Nothing has to cross between parts.
Inputs may be any that keep to these rules, and one draw needn't show every extreme that they name: Each block row names 5 different offsets; block row 0 names 8. `diag_blocks`: each diagonal block is symmetric.
All inputs are finite; a program needn't handle non-finite values.
Results may differ from the reference program's by a relative error of at most 0.0047.
Values may be sent and summed in bfloat16 or wider, within the bound.
A program may use at most 64 MiB of HBM per device.

```python
import math
import jax
import jax.numpy as jnp
from jax import lax

BLOCK_ROWS = 384
NV = 128
BLK_DEV = 2
COUPLED_BLOCKS = 5
HOPS = 4
NB = 32
REACH = 8
ROWS = 12288
STORED_COUNT = 160
N_ATOMS = 4
N_VEC = 2
N_SUB = 2


def draw_diag_blocks(key, part):
    key = jax.random.fold_in(key, 11)
    factor = 0.5 / math.sqrt(BLOCK_ROWS * (1 + 2 * COUPLED_BLOCKS))
    raw = jax.random.normal(key, (NB, BLOCK_ROWS, BLOCK_ROWS), jnp.float32)
    symmetric = (raw + jnp.swapaxes(raw, 1, 2)) * (factor / math.sqrt(2.0))
    return symmetric.astype(jnp.bfloat16)


def draw_offsets(key, part):
    key = jax.random.fold_in(key, 23)
    noise = jax.random.randint(key, (NB, REACH), 0, 1 << 20)
    scores = noise * REACH + jnp.arange(REACH, dtype=jnp.int32)[None, :]
    marker = jnp.zeros((NB, REACH), jnp.int32).at[0, REACH - 1].set(1)
    scores = jnp.where(marker > 0, -1, scores)
    picked = jnp.argsort(scores, axis=1, stable=True)[:, :COUPLED_BLOCKS]
    return (picked + 1).astype(jnp.int32)


def block_scale(rng, dims, shards, least, high):
    gain = 1.0
    for position, shards_of in shards:
        steps = jax.random.uniform(jax.random.fold_in(jax.random.fold_in(rng, 6), position), (shards_of,), jnp.float32, least / len(shards), high / len(shards))
        gain = gain * jnp.repeat(jnp.exp(steps), dims[position] // shards_of).reshape((-1,) + (1,) * (len(dims) - 1 - position))
    return gain


def normal_values(rng, dims, deviation, limit, cuts=(), kind=jnp.bfloat16):
    gain = block_scale(rng, dims, cuts, -0.22, 0.18) if cuts else 1.0
    drawn = jax.random.normal(rng, dims, jnp.float32) * deviation * gain
    return jnp.minimum(jnp.maximum(drawn, -limit), limit).astype(kind)


def setup_inputs(seed: int = 0, part: int = 0) -> dict:
    splits = jax.random.split(jax.random.key(seed), 6)
    part_keys = jax.random.split(jax.random.fold_in(splits[5], part), 6)
    return {
        "t_prev": normal_values(part_keys[0], (NV, ROWS), 1.0, 6.0, ((1, 16),), jnp.float32),
        "t_cur": normal_values(part_keys[1], (NV, ROWS), 1.0, 6.0, ((1, 16),), jnp.float32),
        "diag_blocks": draw_diag_blocks(jax.random.fold_in(jax.random.fold_in(splits[5], part), 71), part),
        "upper_half_blocks": normal_values(part_keys[3], (STORED_COUNT, BLOCK_ROWS, BLOCK_ROWS), (4 * BLOCK_ROWS * (1 + 2 * COUPLED_BLOCKS)) ** -0.5, 0.046875, ((0, 16),)),
        "offsets": draw_offsets(jax.random.fold_in(jax.random.fold_in(splits[5], part), 71), part),
    }


def apply_operator(current, diag_blocks, upper_half_blocks, offsets):
    window = (HOPS + 1) * BLK_DEV
    device_count = N_ATOMS * N_VEC * N_SUB
    block_list = jnp.swapaxes(current.astype(jnp.bfloat16).reshape(NV, NB, BLOCK_ROWS), 0, 1)

    def one_device(accumulated, device):
        first_block = device * BLK_DEV
        own_blocks = lax.dynamic_slice_in_dim(block_list, first_block, BLK_DEV, 0)
        window_ids = ((first_block + jnp.arange(window, dtype=jnp.int32)) % NB).astype(jnp.int32)
        neighbor_blocks = jnp.take(block_list, window_ids, axis=0)
        stored = lax.dynamic_slice_in_dim(upper_half_blocks, first_block * COUPLED_BLOCKS, BLK_DEV * COUPLED_BLOCKS, 0)
        diagonal = lax.dynamic_slice_in_dim(diag_blocks, first_block, BLK_DEV, 0)
        row_offsets = lax.dynamic_slice_in_dim(offsets, first_block, BLK_DEV, 0)
        slot_window = (jnp.arange(BLK_DEV, dtype=jnp.int32)[:, None] + row_offsets).reshape(-1)
        column_blocks = jnp.take(neighbor_blocks, slot_window, axis=0).astype(jnp.float32)
        row_copies = jnp.repeat(own_blocks, COUPLED_BLOCKS, axis=0).astype(jnp.float32)
        stored_f = stored.astype(jnp.float32)
        forward = jnp.einsum('sab,svb->sva', stored_f, column_blocks)
        forward = forward.reshape(BLK_DEV, COUPLED_BLOCKS, NV, BLOCK_ROWS).sum(axis=1)
        forward = forward + jnp.einsum('rab,rvb->rva', diagonal.astype(jnp.float32), own_blocks.astype(jnp.float32))
        transposed = jnp.einsum('sab,sva->svb', stored_f, row_copies)
        onehot = (slot_window[:, None] == jnp.arange(window, dtype=jnp.int32)[None, :]).astype(jnp.float32)
        grouped = jnp.einsum('svb,sw->wvb', transposed, onehot, precision=lax.Precision.HIGHEST)
        grouped = lax.optimization_barrier(grouped.astype(jnp.bfloat16)).astype(jnp.float32)
        owned_indices = (first_block + jnp.arange(BLK_DEV, dtype=jnp.int32)).astype(jnp.int32)
        accumulated = accumulated.at[owned_indices].add(forward)
        accumulated = accumulated.at[window_ids].add(grouped)
        return accumulated, None

    start = jnp.zeros((NB, NV, BLOCK_ROWS), jnp.float32)
    accumulated, _ = lax.scan(one_device, start, jnp.arange(device_count, dtype=jnp.int32))
    return jnp.swapaxes(accumulated, 0, 1).reshape(NV, NB * BLOCK_ROWS)


def reference(t_prev, t_cur, diag_blocks, upper_half_blocks, offsets):
    t_one = 2.0 * apply_operator(t_cur, diag_blocks, upper_half_blocks, offsets) - t_prev
    t_two = 2.0 * apply_operator(t_one, diag_blocks, upper_half_blocks, offsets) - t_cur
    return t_one, t_two
```

```python
import functools

import jax
import jax.numpy as jnp
from jax import lax
from jax.experimental import pallas as pl
from jax.experimental.pallas import tpu as pltpu
from jax.sharding import PartitionSpec as P

HOPS = 4
CHUNKS = 2
AXES = ("grp", "atoms", "vec", "sub")
MESH = pl.DeviceIdType.MESH
F32 = jnp.float32
BF16 = jnp.bfloat16

FAR, NEAR, MATE_NEAR, MATE_FAR, PART_NEAR, PART_FAR, PART_X, PART_Z = range(8)


def kernel(
    n_atoms, n_vec, offsets, t_cur, t_prev_hbm, diag_hbm, stored_hbm, t_one, t_two,
    diag, stored, t_prev, products, sums, own, *rest,
):
    steps = 2 * CHUNKS
    windows, outgoing, incoming = rest[:steps], rest[steps:2 * steps], rest[2 * steps:3 * steps]
    load_sem, send_sem, recv_sem = rest[3 * steps:]
    size = diag.shape[1]
    slots = offsets.shape[1]
    rows = t_cur.shape[0] // CHUNKS
    tree = n_vec == 2

    g, z, x, c = [lax.axis_index(name) for name in AXES]
    chips = n_atoms * n_vec
    place = z * n_vec + x

    def chip(step):
        at = lax.rem(place + step + chips, chips)
        return (g, at // n_vec, lax.rem(at, n_vec), c)

    mate = (g, z, x, 1 - c)
    far_ahead, far_behind = chip(2), chip(-2)
    if tree:
        near_ahead = near_behind = (g, z, 1 - x, c)
        partners = (mate, near_ahead, far_ahead, far_behind)
    else:
        near_ahead, near_behind = chip(1), chip(-1)
        partners = (mate, near_ahead, near_behind, far_ahead, far_behind)

    loads = [
        pltpu.make_async_copy(stored_hbm, stored, load_sem.at[0]),
        pltpu.make_async_copy(diag_hbm, diag, load_sem.at[1]),
        pltpu.make_async_copy(t_prev_hbm, t_prev, load_sem.at[2]),
    ]
    for load in loads:
        load.start()

    barrier = pltpu.get_barrier_semaphore()
    for partner in partners:
        pl.semaphore_signal(barrier, inc=1, device_id=partner, device_id_type=MESH)

    named = [[offsets[r, k] for k in range(slots)] for r in range(2)]
    found = []
    for r in range(2):
        of_row = {}
        for offset in range(1, 2 * HOPS + 1):
            at = jnp.int32(slots)
            for k in range(slots):
                at = jnp.where(named[r][k] == offset, jnp.int32(k), at)
            of_row[offset] = at
        found.append(of_row)
    for r in range(2):
        products[r, slots] = jnp.zeros((rows, size), F32)

    def copies(s):
        window, out, arrive = windows[s], outgoing[s], incoming[s]

        def copy(which, src, dst, device):
            return pltpu.make_async_remote_copy(
                src_ref=src, dst_ref=dst, send_sem=send_sem.at[s, which],
                recv_sem=recv_sem.at[s, which], device_id=device, device_id_type=MESH,
            )

        near_src = 8 * (1 - x) if tree else 0
        return {
            FAR: copy(FAR, window.at[pl.ds(0, 2)], window.at[pl.ds(8, 2)], far_behind),
            NEAR: copy(NEAR, window.at[pl.ds(near_src, 2)], window.at[pl.ds(4, 2)], near_behind),
            MATE_NEAR: copy(MATE_NEAR, window.at[pl.ds(4, 2)], window.at[pl.ds(2 + 4 * c, 2)], mate),
            MATE_FAR: copy(
                MATE_FAR, window.at[pl.ds(8 * (1 - c), 2)], window.at[pl.ds(6 - 4 * c, 2)], mate
            ),
            PART_NEAR: copy(PART_NEAR, out.at[0], arrive.at[0], mate),
            PART_FAR: copy(PART_FAR, out.at[1], arrive.at[1], mate),
            PART_X: copy(PART_X, out.at[2], arrive.at[2], near_ahead),
            PART_Z: copy(PART_Z, out.at[3], arrive.at[3], far_ahead),
        }

    every = [copies(s) for s in range(steps)]

    def send_vectors(s, value):
        windows[s][0] = value[:, :size].astype(BF16)
        windows[s][1] = value[:, size:].astype(BF16)
        every[s][FAR].start()
        if tree:
            @pl.when(x == 1)
            def _():
                every[s][NEAR].start()
        else:
            every[s][NEAR].start()

    def compute_parts(s):
        window, out = windows[s], outgoing[s]
        for r in range(2):
            block = window[r]
            for k in range(slots):
                products[r, k] = jnp.dot(block, stored[r * slots + k], preferred_element_type=F32)

        def part(w):
            total = None
            if 1 <= w <= 2 * HOPS:
                total = products[0, found[0][w]]
            if 1 <= w - 1 <= 2 * HOPS:
                term = products[1, found[1][w - 1]]
                total = term if total is None else total + term
            return total

        near = jnp.where(c == 0, 0, 1)
        for i in range(2):
            one, three = part(2 + i), part(6 + i)
            out[near, i] = three.astype(BF16)
            out[1 - near, i] = one.astype(BF16)
        every[s][PART_NEAR].start()
        every[s][PART_FAR].start()
        for i in range(2):
            sums[s, i] = part(4 + i)
            sums[s, 2 + i] = part(8 + i)
        sums[s, 4] = part(1)

    def join_parts(s):
        out, arrive = outgoing[s], incoming[s]
        every[s][PART_NEAR].wait_recv()
        for i in range(2):
            out[2, i] = (sums[s, i] + arrive[0, i].astype(F32)).astype(BF16)
        every[s][PART_X].start()
        every[s][PART_FAR].wait_recv()
        for i in range(2):
            extra = arrive[1, i].astype(F32)
            sums[s, 2 + i] = sums[s, 2 + i] + jnp.where(c == 0, extra, 0.0)
            extra = jnp.where(c == 1, extra, 0.0)
            own[s, i] = extra + sums[s, 4] if i == 1 else extra
        if tree:
            @pl.when(x == 1)
            def _():
                send_far_part(s, False)
        else:
            send_far_part(s, False)

    def send_far_part(s, add):
        out, arrive = outgoing[s], incoming[s]
        for i in range(2):
            total = sums[s, 2 + i]
            if add:
                total = total + arrive[2, i].astype(F32)
            out[3, i] = total.astype(BF16)
        every[s][PART_Z].start()

    def relay_vectors(s):
        every[s][FAR].wait_recv()
        every[s][MATE_FAR].start()
        if tree:
            @pl.when(x == 0)
            def _():
                every[s][NEAR].start()

    def relay_parts(s):
        if tree:
            @pl.when(x == 0)
            def _():
                every[s][PART_X].wait_recv()
                send_far_part(s, True)

    def spread_vectors(s):
        every[s][NEAR].wait_recv()
        every[s][MATE_NEAR].start()

    def multiply(s):
        every[s][MATE_NEAR].wait_recv()
        every[s][MATE_FAR].wait_recv()
        window = windows[s]
        for r in range(2):
            total = jnp.dot(window[r], diag[r], preferred_element_type=F32)
            for k in range(slots):
                total = total + lax.dot_general(
                    window[r + named[r][k]], stored[r * slots + k],
                    (((1,), (1,)), ((), ())), preferred_element_type=F32,
                )
            own[s, r] = own[s, r] + total

    def finish(s, before, result, part_rows):
        arrive = incoming[s]
        if tree:
            @pl.when(x == 1)
            def _():
                every[s][PART_X].wait_recv()
        else:
            every[s][PART_X].wait_recv()
        every[s][PART_Z].wait_recv()
        for r in range(2):
            total = own[s, r] + arrive[3, r].astype(F32)
            near = arrive[2, r].astype(F32)
            total = total + (jnp.where(x == 1, near, 0.0) if tree else near)
            cols = pl.ds(r * size, size)
            result[part_rows, cols] = 2.0 * total - before[part_rows, cols]

    chunk_rows = [pl.ds(h * rows, rows) for h in range(CHUNKS)]
    first = list(range(CHUNKS))
    second = [CHUNKS + h for h in first]

    pl.semaphore_wait(barrier, len(partners))
    for h in first:
        send_vectors(h, t_cur[chunk_rows[h], :])
    loads[0].wait()
    for h in first:
        compute_parts(h)
    for h in first:
        join_parts(h)
    loads[1].wait()
    loads[2].wait()
    for h in first:
        relay_vectors(h)
        relay_parts(h)
    for h in first:
        spread_vectors(h)
    for h in first:
        multiply(h)
        finish(h, t_prev, t_one, chunk_rows[h])
        s = second[h]
        send_vectors(s, t_one[chunk_rows[h], :])
        compute_parts(s)
        join_parts(s)
    for h in first:
        relay_vectors(second[h])
        relay_parts(second[h])
    for h in first:
        spread_vectors(second[h])
    for h in first:
        multiply(second[h])
        finish(second[h], t_cur, t_two, chunk_rows[h])
    for s in range(steps):
        for copy in every[s].values():
            copy.wait_send()


def solution(mesh):
    n_atoms, n_vec = mesh.shape["atoms"], mesh.shape["vec"]

    def local(t_prev, t_cur, diag_blocks, upper_half_blocks, offsets):
        rows = t_cur.shape[0] // CHUNKS
        size = diag_blocks.shape[1]
        slots = offsets.shape[1]
        steps = 2 * CHUNKS
        vmem = pl.BlockSpec(memory_space=pltpu.VMEM)
        hbm = pl.BlockSpec(memory_space=pl.ANY)
        return pl.pallas_call(
            functools.partial(kernel, n_atoms, n_vec),
            out_shape=(
                jax.ShapeDtypeStruct(t_cur.shape, F32), jax.ShapeDtypeStruct(t_cur.shape, F32)
            ),
            in_specs=[pl.BlockSpec(memory_space=pltpu.SMEM), vmem, hbm, hbm, hbm],
            out_specs=(vmem, vmem),
            scratch_shapes=[
                pltpu.VMEM(diag_blocks.shape, BF16),
                pltpu.VMEM(upper_half_blocks.shape, BF16),
                pltpu.VMEM(t_prev.shape, F32),
                pltpu.VMEM((2, slots + 1, rows, size), F32),
                pltpu.VMEM((steps, 5, rows, size), F32),
                pltpu.VMEM((steps, 2, rows, size), F32),
                *[pltpu.VMEM((2 * HOPS + 2, rows, size), BF16) for _ in range(steps)],
                *[pltpu.VMEM((4, 2, rows, size), BF16) for _ in range(2 * steps)],
                pltpu.SemaphoreType.DMA((3,)),
                pltpu.SemaphoreType.DMA((steps, 8)),
                pltpu.SemaphoreType.DMA((steps, 8)),
            ],
            compiler_params=pltpu.CompilerParams(
                collective_id=0, has_side_effects=True, vmem_limit_bytes=48 << 20
            ),
        )(offsets, t_cur, t_prev, diag_blocks, upper_half_blocks)

    in_specs = (
        P("grp", ("atoms", "vec", "sub")),
        P("grp", ("atoms", "vec", "sub")),
        P(AXES, None, None),
        P(AXES, None, None),
        P(AXES, None),
    )
    out_specs = (P("grp", ("atoms", "vec", "sub")), P("grp", ("atoms", "vec", "sub")))
    return jax.shard_map(local, mesh=mesh, in_specs=in_specs, out_specs=out_specs, check_vma=False)
```

```python
import functools

import jax
import jax.numpy as jnp
from jax import lax
from jax.experimental import pallas as pl
from jax.experimental.pallas import tpu as pltpu
from jax.sharding import PartitionSpec as P

HOPS = 4
CHUNKS = 2
PIECES = 2
AXES = ("grp", "atoms", "vec", "sub")
MESH = pl.DeviceIdType.MESH
F32 = jnp.float32
BF16 = jnp.bfloat16

FAR, NEAR, MATE_NEAR, MATE_FAR, PART_NEAR, PART_FAR, PART_X, PART_Z = range(8)


def kernel(
    n_atoms, n_vec, offsets_hbm, t_cur_hbm, t_prev_hbm, diag_hbm, stored_hbm, t_one, t_two,
    offsets, t_cur, t_prev, diag, stored, sums, own, *rest,
):
    steps = 2 * CHUNKS
    windows, outgoing, incoming = rest[:steps], rest[steps:2 * steps], rest[2 * steps:3 * steps]
    load_sem, send_sem, recv_sem = rest[3 * steps:]
    size = diag.shape[1]
    slots = offsets.shape[1]
    rows = t_cur.shape[0] // CHUNKS
    tree = n_vec == 2

    g, z, x, c = [lax.axis_index(name) for name in AXES]
    chips = n_atoms * n_vec
    place = z * n_vec + x

    def chip(step):
        at = lax.rem(place + step + chips, chips)
        return (g, at // n_vec, lax.rem(at, n_vec), c)

    mate = (g, z, x, 1 - c)
    far_ahead, far_behind = chip(2), chip(-2)
    if tree:
        near_ahead = near_behind = (g, z, 1 - x, c)
        partners = (mate, near_ahead, far_ahead, far_behind)
    else:
        near_ahead, near_behind = chip(1), chip(-1)
        partners = (mate, near_ahead, near_behind, far_ahead, far_behind)

    sources = (t_cur_hbm, offsets_hbm, stored_hbm.at[pl.ds(0, slots)],
               stored_hbm.at[pl.ds(slots, slots)], diag_hbm, t_prev_hbm)
    targets = (t_cur, offsets, stored.at[pl.ds(0, slots)],
               stored.at[pl.ds(slots + 1, slots)], diag, t_prev)
    loads = [
        pltpu.make_async_copy(source, target, load_sem.at[i])
        for i, (source, target) in enumerate(zip(sources, targets))
    ]
    for load in loads:
        load.start()

    barrier = pltpu.get_barrier_semaphore()
    for partner in partners:
        pl.semaphore_signal(barrier, inc=1, device_id=partner, device_id_type=MESH)
    for r in range(2):
        stored[r * (slots + 1) + slots] = jnp.zeros((size, size), BF16)

    def copies(s):
        window, out, arrive = windows[s], outgoing[s], incoming[s]

        def copy(which, src, dst, device):
            return pltpu.make_async_remote_copy(
                src_ref=src, dst_ref=dst, send_sem=send_sem.at[s, which],
                recv_sem=recv_sem.at[s, which], device_id=device, device_id_type=MESH,
            )

        near_src = 4 * (1 - x) if tree else 0
        at = lambda first: window.at[pl.ds(first, 2)]
        return {
            FAR: copy(FAR, at(0), at(4), far_behind),
            NEAR: copy(NEAR, at(near_src), at(2), near_behind),
            MATE_NEAR: copy(MATE_NEAR, at(2), at(6), mate),
            MATE_FAR: copy(MATE_FAR, at(4 * (1 - c)), at(8), mate),
            PART_NEAR: copy(PART_NEAR, out.at[0], arrive.at[0], mate),
            PART_FAR: copy(PART_FAR, out.at[1], arrive.at[1], mate),
            PART_X: copy(PART_X, out.at[2], arrive.at[2], near_ahead),
            PART_Z: copy(PART_Z, out.at[3], arrive.at[3], far_ahead),
        }

    every = [copies(s) for s in range(steps)]

    def only(condition, action):
        if tree:
            pl.when(condition)(action)
        else:
            action()

    def block(r, w):
        return table[r][w - r]

    def send_vectors(s, load):
        windows[s][0] = load(0).astype(BF16)
        windows[s][1] = load(1).astype(BF16)
        every[s][FAR].start()
        only(x == 1, every[s][NEAR].start)

    def part(s, first, second):
        total = None
        for r, at in ((0, first), (1, second)):
            if at is not None:
                term = jnp.dot(windows[s][r], stored[at], preferred_element_type=F32)
                total = term if total is None else total + term
        return total

    def mate_parts(s):
        out = outgoing[s]
        for i in range(2):
            out[0, i] = part(s, *[pick(block(r, 6 + i), block(r, 2 + i)) for r in range(2)]).astype(BF16)
        every[s][PART_NEAR].start()
        for i in range(2):
            out[1, i] = part(s, *[pick(block(r, 2 + i), block(r, 6 + i)) for r in range(2)]).astype(BF16)
        every[s][PART_FAR].start()

    def pick(even, odd):
        return jnp.where(c == 0, even, odd)

    def own_parts(s):
        for i in range(2):
            sums[s, i] = part(s, block(0, 4 + i), block(1, 4 + i))
        sums[s, 2] = part(s, block(0, 8), block(1, 8))
        sums[s, 3] = part(s, None, block(1, 9))

    def own_terms(s):
        own[s, 1] = part(s, block(0, 1), None) + jnp.dot(
            windows[s][1], diag[1], preferred_element_type=F32
        )
        own[s, 0] = jnp.dot(windows[s][0], diag[0], preferred_element_type=F32) + forward(
            s, 1, block(0, 1)
        )

    def forward(s, slot, at):
        return lax.dot_general(
            windows[s][slot], stored[at], (((1,), (1,)), ((), ())), preferred_element_type=F32
        )

    def join_parts(s):
        out, arrive = outgoing[s], incoming[s]
        every[s][PART_NEAR].wait_recv()
        for i in range(2):
            out[2, i] = (sums[s, i] + arrive[0, i].astype(F32)).astype(BF16)
        every[s][PART_X].start()
        every[s][PART_FAR].wait_recv()
        for i in range(2):
            extra = arrive[1, i].astype(F32)
            sums[s, 2 + i] = sums[s, 2 + i] + jnp.where(c == 0, extra, 0.0)
        only(x == 1, lambda: send_far_part(s, False))

    def send_far_part(s, add):
        out, arrive = outgoing[s], incoming[s]
        for i in range(2):
            total = sums[s, 2 + i]
            if add:
                total = total + arrive[2, i].astype(F32)
            out[3, i] = total.astype(BF16)
        every[s][PART_Z].start()

    def relay_vectors(s):
        every[s][FAR].wait_recv()
        if tree:
            pl.when(x == 0)(every[s][NEAR].start)
        every[s][MATE_FAR].start()

    def relay_parts(s, condition):
        if tree:
            @pl.when(jnp.logical_and(x == 0, condition))
            def _():
                every[s][PART_X].wait_recv()
                send_far_part(s, True)

    def add_pair(s, slot, at):
        for r in range(2):
            own[s, r] = own[s, r] + forward(s, slot, at[r][0]) + forward(s, slot + 1, at[r][1])

    def far_terms(s):
        own[s, 0] = own[s, 0] + forward(s, 4, block(0, 8))
        own[s, 1] = own[s, 1] + forward(s, 4, block(1, 8)) + forward(s, 5, block(1, 9))

    def spread_vectors(s):
        every[s][NEAR].wait_recv()
        every[s][MATE_NEAR].start()

    def near_terms(s):
        add_pair(s, 2, [[block(r, 4), block(r, 5)] for r in range(2)])

    def mate_far_terms(s):
        every[s][MATE_FAR].wait_recv()
        add_pair(s, 8, [[pick(block(r, 2 + i), block(r, 6 + i)) for i in range(2)] for r in range(2)])

    def mate_near_terms(s):
        every[s][MATE_NEAR].wait_recv()
        add_pair(s, 6, [[pick(block(r, 6 + i), block(r, 2 + i)) for i in range(2)] for r in range(2)])

    def finish(s, before, result, part_rows):
        arrive = incoming[s]
        only(x == 1, every[s][PART_X].wait_recv)
        every[s][PART_Z].wait_recv()
        for r in range(2):
            total = own[s, r] + arrive[3, r].astype(F32)
            total = total + jnp.where(c == 1, arrive[1, r].astype(F32), 0.0)
            near = arrive[2, r].astype(F32)
            total = total + (jnp.where(x == 1, near, 0.0) if tree else near)
            cols = pl.ds(r * size, size)
            result[part_rows, cols] = 2.0 * total - before[part_rows, cols]

    chunk_rows = [pl.ds(h * rows, rows) for h in range(CHUNKS)]
    first = list(range(CHUNKS))
    second = [CHUNKS + h for h in first]
    last = z == n_atoms - 1

    def columns(ref, h):
        return lambda r: ref[chunk_rows[h], pl.ds(r * size, size)]

    def middle(group):
        for s in group:
            relay_parts(s, last)
        for s in group:
            relay_vectors(s)
            relay_parts(s, jnp.logical_not(last))

    def gather(s):
        far_terms(s)
        spread_vectors(s)
        near_terms(s)
        mate_far_terms(s)
        mate_near_terms(s)

    loads[0].wait()
    pl.semaphore_wait(barrier, len(partners))
    for h in first:
        send_vectors(h, columns(t_cur, h))
    loads[1].wait()
    table = []
    for r in range(2):
        of_row = {}
        for offset in range(1, 2 * HOPS + 1):
            at = jnp.int32(slots)
            for k in range(slots):
                at = jnp.where(offsets[r, k] == offset, jnp.int32(k), at)
            of_row[offset] = at + r * (slots + 1)
        table.append(of_row)
    loads[2].wait()
    loads[3].wait()
    for h in first:
        mate_parts(h)
        own_parts(h)
        join_parts(h)
    loads[4].wait()
    for h in first:
        own_terms(h)
    loads[5].wait()
    middle(first)
    for h in first:
        gather(h)
        finish(h, t_prev, t_one, chunk_rows[h])
        s = second[h]
        send_vectors(s, columns(t_one, h))
        mate_parts(s)
        own_parts(s)
        join_parts(s)
        own_terms(s)
    middle(second)
    for h in first:
        gather(second[h])
        finish(second[h], t_cur, t_two, chunk_rows[h])
    for s in range(steps):
        for copy in every[s].values():
            copy.wait_send()


def deliver(one, two, one_out, two_out, held, sems):
    rows = one.shape[0] // PIECES
    stages = []
    for i, (source, target) in enumerate(((one, one_out), (two, two_out))):
        for p in range(PIECES):
            part = pl.ds(p * rows, rows)
            stages.append((
                pltpu.make_async_copy(source.at[part], held.at[i, part], sems.at[0, i, p]),
                pltpu.make_async_copy(held.at[i, part], target.at[part], sems.at[1, i, p]),
            ))
    for load, _ in stages:
        load.start()
    for load, store in stages:
        load.wait()
        store.start()
    for _, store in stages:
        store.wait()


def solution(mesh):
    n_atoms, n_vec = mesh.shape["atoms"], mesh.shape["vec"]

    def local(t_prev, t_cur, diag_blocks, upper_half_blocks, offsets):
        rows = t_cur.shape[0] // CHUNKS
        size = diag_blocks.shape[1]
        slots = offsets.shape[1]
        steps = 2 * CHUNKS
        vmem = pl.BlockSpec(memory_space=pltpu.VMEM)
        hbm = pl.BlockSpec(memory_space=pltpu.HBM)
        results = pl.pallas_call(
            functools.partial(kernel, n_atoms, n_vec),
            out_shape=(
                jax.ShapeDtypeStruct(t_cur.shape, F32), jax.ShapeDtypeStruct(t_cur.shape, F32)
            ),
            in_specs=[hbm] * 5,
            out_specs=(vmem, vmem),
            scratch_shapes=[
                pltpu.SMEM(offsets.shape, jnp.int32),
                pltpu.VMEM(t_cur.shape, F32),
                pltpu.VMEM(t_prev.shape, F32),
                pltpu.VMEM(diag_blocks.shape, BF16),
                pltpu.VMEM((2 * (slots + 1), size, size), BF16),
                pltpu.VMEM((steps, 4, rows, size), F32),
                pltpu.VMEM((steps, 2, rows, size), F32),
                *[pltpu.VMEM((2 * HOPS + 2, rows, size), BF16) for _ in range(steps)],
                *[pltpu.VMEM((4, 2, rows, size), BF16) for _ in range(2 * steps)],
                pltpu.SemaphoreType.DMA((6,)),
                pltpu.SemaphoreType.DMA((steps, 8)),
                pltpu.SemaphoreType.DMA((steps, 8)),
            ],
            compiler_params=pltpu.CompilerParams(
                collective_id=0, has_side_effects=True, vmem_limit_bytes=62 << 20
            ),
        )(offsets, t_cur, t_prev, diag_blocks, upper_half_blocks)
        return pl.pallas_call(
            deliver,
            out_shape=tuple(jax.ShapeDtypeStruct(a.shape, a.dtype) for a in results),
            in_specs=[pl.BlockSpec(memory_space=pl.ANY)] * 2,
            out_specs=(hbm, hbm),
            scratch_shapes=[pltpu.VMEM((2, *t_cur.shape), F32), pltpu.SemaphoreType.DMA((2, 2, PIECES))],
        )(*results)

    in_specs = (
        P("grp", ("atoms", "vec", "sub")),
        P("grp", ("atoms", "vec", "sub")),
        P(AXES, None, None),
        P(AXES, None, None),
        P(AXES, None),
    )
    out_specs = (P("grp", ("atoms", "vec", "sub")), P("grp", ("atoms", "vec", "sub")))
    return jax.shard_map(local, mesh=mesh, in_specs=in_specs, out_specs=out_specs, check_vma=False)
```

```python
import functools

import jax
import jax.numpy as jnp
from jax import lax
from jax.experimental import pallas as pl
from jax.experimental.pallas import tpu as pltpu
from jax.sharding import PartitionSpec as P

HOPS = 4
CHUNKS = 2
AXES = ("grp", "atoms", "vec", "sub")
MESH = pl.DeviceIdType.MESH
F32 = jnp.float32
BF16 = jnp.bfloat16

FAR, NEAR, MATE_NEAR, MATE_FAR, PART_NEAR, PART_FAR, PART_X, PART_Z = range(8)


def kernel(
    n_atoms, n_vec, offsets_hbm, t_cur_hbm, t_prev_hbm, diag_hbm, stored_hbm, t_one, t_two,
    offsets, t_cur, t_prev, diag, stored, sums, own, *rest,
):
    steps = 2 * CHUNKS
    windows, outgoing, incoming = rest[:steps], rest[steps:2 * steps], rest[2 * steps:3 * steps]
    load_sem, send_sem, recv_sem = rest[3 * steps:]
    size = diag.shape[1]
    slots = offsets.shape[1]
    rows = t_cur.shape[0] // CHUNKS
    tree = n_vec == 2

    g, z, x, c = [lax.axis_index(name) for name in AXES]
    chips = n_atoms * n_vec
    place = z * n_vec + x

    def chip(step):
        at = lax.rem(place + step + chips, chips)
        return (g, at // n_vec, lax.rem(at, n_vec), c)

    mate = (g, z, x, 1 - c)
    far_ahead, far_behind = chip(2), chip(-2)
    if tree:
        near_ahead = near_behind = (g, z, 1 - x, c)
        partners = (mate, near_ahead, far_ahead, far_behind)
    else:
        near_ahead, near_behind = chip(1), chip(-1)
        partners = (mate, near_ahead, near_behind, far_ahead, far_behind)

    sources = (t_cur_hbm, offsets_hbm, stored_hbm.at[pl.ds(0, slots)],
               stored_hbm.at[pl.ds(slots, slots)], diag_hbm, t_prev_hbm)
    targets = (t_cur, offsets, stored.at[pl.ds(0, slots)],
               stored.at[pl.ds(slots + 1, slots)], diag, t_prev)
    loads = [
        pltpu.make_async_copy(source, target, load_sem.at[i])
        for i, (source, target) in enumerate(zip(sources, targets))
    ]
    for load in loads:
        load.start()

    barrier = pltpu.get_barrier_semaphore()
    for partner in partners:
        pl.semaphore_signal(barrier, inc=1, device_id=partner, device_id_type=MESH)
    for r in range(2):
        stored[r * (slots + 1) + slots] = jnp.zeros((size, size), BF16)

    def copies(s):
        window, out, arrive = windows[s], outgoing[s], incoming[s]

        def copy(which, src, dst, device):
            return pltpu.make_async_remote_copy(
                src_ref=src, dst_ref=dst, send_sem=send_sem.at[s, which],
                recv_sem=recv_sem.at[s, which], device_id=device, device_id_type=MESH,
            )

        near_src = 4 * (1 - x) if tree else 0
        at = lambda first: window.at[pl.ds(first, 2)]
        return {
            FAR: copy(FAR, at(0), at(4), far_behind),
            NEAR: copy(NEAR, at(near_src), at(2), near_behind),
            MATE_NEAR: copy(MATE_NEAR, at(2), at(6), mate),
            MATE_FAR: copy(MATE_FAR, at(4 * (1 - c)), at(8), mate),
            PART_NEAR: copy(PART_NEAR, out.at[0], arrive.at[0], mate),
            PART_FAR: copy(PART_FAR, out.at[1], arrive.at[1], mate),
            PART_X: copy(PART_X, out.at[2], arrive.at[2], near_ahead),
            PART_Z: copy(PART_Z, out.at[3], arrive.at[3], far_ahead),
        }

    every = [copies(s) for s in range(steps)]

    def only(condition, action):
        if tree:
            pl.when(condition)(action)
        else:
            action()

    def block(r, w):
        return table[r][w - r]

    def send_vectors(s, load):
        windows[s][0] = load(0).astype(BF16)
        windows[s][1] = load(1).astype(BF16)
        every[s][FAR].start()
        only(x == 1, every[s][NEAR].start)

    def part(s, first, second):
        total = None
        for r, at in ((0, first), (1, second)):
            if at is not None:
                term = jnp.dot(windows[s][r], stored[at], preferred_element_type=F32)
                total = term if total is None else total + term
        return total

    def mate_parts(s):
        out = outgoing[s]
        for i in range(2):
            out[0, i] = part(s, *[pick(block(r, 6 + i), block(r, 2 + i)) for r in range(2)]).astype(BF16)
        every[s][PART_NEAR].start()
        for i in range(2):
            out[1, i] = part(s, *[pick(block(r, 2 + i), block(r, 6 + i)) for r in range(2)]).astype(BF16)
        every[s][PART_FAR].start()

    def pick(even, odd):
        return jnp.where(c == 0, even, odd)

    def own_parts(s):
        for i in range(2):
            sums[s, i] = part(s, block(0, 4 + i), block(1, 4 + i))
        sums[s, 2] = part(s, block(0, 8), block(1, 8))
        sums[s, 3] = part(s, None, block(1, 9))

    def own_terms(s):
        own[s, 1] = part(s, block(0, 1), None) + jnp.dot(
            windows[s][1], diag[1], preferred_element_type=F32
        )
        own[s, 0] = jnp.dot(windows[s][0], diag[0], preferred_element_type=F32) + forward(
            s, 1, block(0, 1)
        )

    def forward(s, slot, at):
        return lax.dot_general(
            windows[s][slot], stored[at], (((1,), (1,)), ((), ())), preferred_element_type=F32
        )

    def join_parts(s):
        out, arrive = outgoing[s], incoming[s]
        every[s][PART_NEAR].wait_recv()
        for i in range(2):
            out[2, i] = (sums[s, i] + arrive[0, i].astype(F32)).astype(BF16)
        every[s][PART_X].start()
        every[s][PART_FAR].wait_recv()
        for i in range(2):
            extra = arrive[1, i].astype(F32)
            sums[s, 2 + i] = sums[s, 2 + i] + jnp.where(c == 0, extra, 0.0)
        only(x == 1, lambda: send_far_part(s, False))

    def send_far_part(s, add):
        out, arrive = outgoing[s], incoming[s]
        for i in range(2):
            total = sums[s, 2 + i]
            if add:
                total = total + arrive[2, i].astype(F32)
            out[3, i] = total.astype(BF16)
        every[s][PART_Z].start()

    def relay_vectors(s):
        every[s][FAR].wait_recv()
        if tree:
            pl.when(x == 0)(every[s][NEAR].start)
        every[s][MATE_FAR].start()

    def relay_parts(s, condition):
        if tree:
            @pl.when(jnp.logical_and(x == 0, condition))
            def _():
                every[s][PART_X].wait_recv()
                send_far_part(s, True)

    def add_pair(s, slot, at):
        for r in range(2):
            own[s, r] = own[s, r] + forward(s, slot, at[r][0]) + forward(s, slot + 1, at[r][1])

    def far_terms(s):
        own[s, 0] = own[s, 0] + forward(s, 4, block(0, 8))
        own[s, 1] = own[s, 1] + forward(s, 4, block(1, 8)) + forward(s, 5, block(1, 9))

    def spread_vectors(s):
        every[s][NEAR].wait_recv()
        every[s][MATE_NEAR].start()

    def near_terms(s):
        add_pair(s, 2, [[block(r, 4), block(r, 5)] for r in range(2)])

    def mate_far_terms(s):
        every[s][MATE_FAR].wait_recv()
        add_pair(s, 8, [[pick(block(r, 2 + i), block(r, 6 + i)) for i in range(2)] for r in range(2)])

    def mate_near_terms(s):
        every[s][MATE_NEAR].wait_recv()
        add_pair(s, 6, [[pick(block(r, 6 + i), block(r, 2 + i)) for i in range(2)] for r in range(2)])

    def finish(s, before, result, part_rows):
        arrive = incoming[s]
        only(x == 1, every[s][PART_X].wait_recv)
        every[s][PART_Z].wait_recv()
        for r in range(2):
            total = own[s, r] + arrive[3, r].astype(F32)
            total = total + jnp.where(c == 1, arrive[1, r].astype(F32), 0.0)
            near = arrive[2, r].astype(F32)
            total = total + (jnp.where(x == 1, near, 0.0) if tree else near)
            cols = pl.ds(r * size, size)
            result[part_rows, cols] = 2.0 * total - before[part_rows, cols]

    chunk_rows = [pl.ds(h * rows, rows) for h in range(CHUNKS)]
    first = list(range(CHUNKS))
    second = [CHUNKS + h for h in first]
    last = z == n_atoms - 1

    def columns(ref, h):
        return lambda r: ref[chunk_rows[h], pl.ds(r * size, size)]

    def middle(group):
        for s in group:
            relay_parts(s, last)
        for s in group:
            relay_vectors(s)
            relay_parts(s, jnp.logical_not(last))

    def gather(s):
        far_terms(s)
        spread_vectors(s)
        near_terms(s)
        mate_far_terms(s)
        mate_near_terms(s)

    loads[0].wait()
    pl.semaphore_wait(barrier, len(partners))
    for h in first:
        send_vectors(h, columns(t_cur, h))
    loads[1].wait()
    table = []
    for r in range(2):
        of_row = {}
        for offset in range(1, 2 * HOPS + 1):
            at = jnp.int32(slots)
            for k in range(slots):
                at = jnp.where(offsets[r, k] == offset, jnp.int32(k), at)
            of_row[offset] = at + r * (slots + 1)
        table.append(of_row)
    loads[2].wait()
    loads[3].wait()
    for h in first:
        mate_parts(h)
        own_parts(h)
        join_parts(h)
    loads[4].wait()
    for h in first:
        own_terms(h)
    loads[5].wait()
    middle(first)
    for h in first:
        gather(h)
        finish(h, t_prev, t_one, chunk_rows[h])
        s = second[h]
        send_vectors(s, columns(t_one, h))
        mate_parts(s)
        own_parts(s)
        join_parts(s)
        own_terms(s)
    middle(second)
    for h in first:
        gather(second[h])
        finish(second[h], t_cur, t_two, chunk_rows[h])
    for s in range(steps):
        for copy in every[s].values():
            copy.wait_send()


def deliver(one, two, one_out, two_out, sems):
    copies = [
        pltpu.make_async_copy(one, one_out, sems.at[0]),
        pltpu.make_async_copy(two, two_out, sems.at[1]),
    ]
    for copy in copies:
        copy.start()
    for copy in copies:
        copy.wait()


def solution(mesh):
    n_atoms, n_vec = mesh.shape["atoms"], mesh.shape["vec"]

    def local(t_prev, t_cur, diag_blocks, upper_half_blocks, offsets):
        rows = t_cur.shape[0] // CHUNKS
        size = diag_blocks.shape[1]
        slots = offsets.shape[1]
        steps = 2 * CHUNKS
        vmem = pl.BlockSpec(memory_space=pltpu.VMEM)
        hbm = pl.BlockSpec(memory_space=pltpu.HBM)
        results = pl.pallas_call(
            functools.partial(kernel, n_atoms, n_vec),
            out_shape=(
                jax.ShapeDtypeStruct(t_cur.shape, F32), jax.ShapeDtypeStruct(t_cur.shape, F32)
            ),
            in_specs=[hbm] * 5,
            out_specs=(vmem, vmem),
            scratch_shapes=[
                pltpu.SMEM(offsets.shape, jnp.int32),
                pltpu.VMEM(t_cur.shape, F32),
                pltpu.VMEM(t_prev.shape, F32),
                pltpu.VMEM(diag_blocks.shape, BF16),
                pltpu.VMEM((2 * (slots + 1), size, size), BF16),
                pltpu.VMEM((steps, 4, rows, size), F32),
                pltpu.VMEM((steps, 2, rows, size), F32),
                *[pltpu.VMEM((2 * HOPS + 2, rows, size), BF16) for _ in range(steps)],
                *[pltpu.VMEM((4, 2, rows, size), BF16) for _ in range(2 * steps)],
                pltpu.SemaphoreType.DMA((6,)),
                pltpu.SemaphoreType.DMA((steps, 8)),
                pltpu.SemaphoreType.DMA((steps, 8)),
            ],
            compiler_params=pltpu.CompilerParams(
                collective_id=0, has_side_effects=True, vmem_limit_bytes=58 << 20
            ),
        )(offsets, t_cur, t_prev, diag_blocks, upper_half_blocks)
        return pl.pallas_call(
            deliver,
            out_shape=tuple(jax.ShapeDtypeStruct(a.shape, a.dtype) for a in results),
            in_specs=[vmem] * 2,
            out_specs=(hbm, hbm),
            scratch_shapes=[pltpu.SemaphoreType.DMA((2,))],
        )(*results)

    in_specs = (
        P("grp", ("atoms", "vec", "sub")),
        P("grp", ("atoms", "vec", "sub")),
        P(AXES, None, None),
        P(AXES, None, None),
        P(AXES, None),
    )
    out_specs = (P("grp", ("atoms", "vec", "sub")), P("grp", ("atoms", "vec", "sub")))
    return jax.shard_map(local, mesh=mesh, in_specs=in_specs, out_specs=out_specs, check_vma=False)
```
